32 devices in a mesh: ctx: 16 (over z, y, core), exp: 2 (over x).
Axes of the slice: x: 2, y: 2, z: 4, core: 2. Of those that a mesh axis runs over, the one named last changes fastest.
Arguments:
- queries: bfloat16 [2, 2048, 2048], P('exp', 'ctx'), may hold values from -64 to 64
- rotated_key_rows: bfloat16 [2, 2048, 256], P('exp', 'ctx'), may hold values from -7 to 7
- value_row_array: bfloat16 [2, 2048, 256], P('exp', 'ctx'), may hold values from -6 to 6
- residual: bfloat16 [2, 2048, 2048], P('exp', 'ctx'), may hold values from -40 to 40
- norm_gain: float32 [2048], replicated, may hold values from 0.1 to 1.9
- expert_ids: int32 [2, 2048, 1], P('exp', 'ctx'), may hold values from 0 to 7; in each aligned block of 128 rows (0 to 127, 128 to 255, ..., all dimensions but the last counted through in order) at most 32 rows name the same one
- gate_values: float32 [2, 2048, 1], P('exp', 'ctx'), may hold values from 0.25 to 1
- w_gate_up: bfloat16 [16, 2, 2, 192, 2048], P('ctx', 'exp'), may hold values from -0.125 to 0.125
- w_down: bfloat16 [16, 2, 192, 2048], P('ctx', 'exp'), may hold values from -0.21875 to 0.21875
Outputs:
- layer_out: bfloat16 [2, 2048, 2048], P('exp', 'ctx')
The draws below stay inside these ranges and needn't reach their ends.
Inputs may be any that keep to these rules, and one draw needn't show every extreme that they name: `expert_ids`: among the rows of one device (aligned blocks of 128 tokens along the second dimension) no expert is named more than 32 times, a bound that some block reaches.
All inputs are finite; a program needn't handle non-finite values.
Results may differ from the reference program's by a relative error of at most 0.013.
Values may be sent and summed in bfloat16 or wider, within the bound.
A program may use at most 64 MiB of HBM per device.

```python
import math
import jax
import jax.numpy as jnp
import numpy as np
from jax import lax

D = 2048
HID = 768
QUERY_HEADS = 16
KEY_VALUE_HEADS = 2
HEAD_SIZE = 128
TOP = 1
TOK_DEV = 128
EPG = 4
EXPERTS = 8
QUARTER = 192
GROUP_TOKENS = 2048
PROMPT_LENGTH = 1024
MOST = 32
N_CTX = 16
N_EXP = 2


def pair_fields(key):
    query_key = jax.random.fold_in(key, 11)
    keys_random_key = jax.random.fold_in(key, 12)
    key_head_rows = 1.5 * jnp.clip(jax.random.normal(keys_random_key, (N_EXP, GROUP_TOKENS, KEY_VALUE_HEADS, HEAD_SIZE), jnp.float32), -4.0, 4.0)
    query_head_rows = 1.5 * jnp.clip(jax.random.normal(query_key, (N_EXP, GROUP_TOKENS, QUERY_HEADS, HEAD_SIZE), jnp.float32), -4.0, 4.0)
    return (query_head_rows.reshape(N_EXP, GROUP_TOKENS, QUERY_HEADS * HEAD_SIZE), key_head_rows.reshape(N_EXP, GROUP_TOKENS, KEY_VALUE_HEADS * HEAD_SIZE))


def draw_queries(key, part):
    return pair_fields(key)[0].astype(jnp.bfloat16)


def draw_rotated_key_rows(key, part):
    return pair_fields(key)[1].astype(jnp.bfloat16)


def draw_residual(key, part):
    base_key = jax.random.fold_in(key, 21)
    row_key = jax.random.fold_in(key, 22)
    column_key = jax.random.fold_in(key, 23)
    column_scale = jnp.exp(jax.random.uniform(column_key, (1, 1, D), jnp.float32, math.log(0.3), math.log(3.0)))
    row_scale = jnp.exp(jax.random.uniform(row_key, (N_EXP, GROUP_TOKENS, 1), jnp.float32, math.log(0.3), math.log(3.0)))
    base = jnp.clip(jax.random.normal(base_key, (N_EXP, GROUP_TOKENS, D), jnp.float32), -4.0, 4.0)
    return (base * row_scale * column_scale).astype(jnp.bfloat16)


def shard_levels(own_key, extent, pieces, smallest, high):
    gain = 1.0
    for dim, shards_of in pieces:
        steps = jax.random.uniform(jax.random.fold_in(jax.random.fold_in(own_key, 6), dim), (shards_of,), jnp.float32, smallest / len(pieces), high / len(pieces))
        gain = gain * jnp.repeat(jnp.exp(steps), extent[dim] // shards_of).reshape((-1,) + (1,) * (len(extent) - 1 - dim))
    return gain


def assign_block(key, own, number, rows, amount, top, limit, slope):
    order = jax.random.permutation(key, amount)
    crowded, usual = shares(amount, rows * top, limit, slope, True), shares(amount, rows * top, limit, slope, False)
    places = jnp.arange(amount)

    def named(lengths, rotation):
        used = int((lengths > 0).sum())
        fixed = max(1, used // 4)
        moved = fixed + (places - fixed + rotation * (used - fixed)) % max(1, amount - fixed)
        return jnp.zeros((amount,), jnp.int32).at[order[jnp.where(places < fixed, places, moved)]].set(jnp.asarray(lengths, jnp.int32))

    lengths = jnp.where(number % 4 == 0, named(crowded, number // 4), named(usual, number - number // 4 - 1))
    mixed = jax.random.permutation(jax.random.fold_in(own, 3), amount)
    donor, sink = mixed[0:amount // 2 * 2:2], mixed[1:amount // 2 * 2:2]
    room = jnp.minimum(lengths[donor] - 1, limit - lengths[sink]) // 2
    room = jnp.where((donor == order[0]) | (sink == order[0]) | (lengths[sink] == 0), 0, jnp.maximum(room, 0))
    moved = jax.random.randint(jax.random.fold_in(own, 4), (amount // 2,), 0, 1 << 20) % (room + 1)
    lengths = lengths.at[donor].add(-moved).at[sink].add(moved)
    labels = jnp.searchsorted(jnp.cumsum(lengths), jnp.arange(rows * top), side="right").astype(jnp.int32)
    listing = labels.reshape(top, rows).T
    listing = listing[jax.random.permutation(jax.random.fold_in(own, 1), rows)]
    rotation = jax.random.randint(jax.random.fold_in(own, 2), (rows, 1), 0, top)
    return jnp.take_along_axis(listing, (jnp.arange(top)[None, :] + rotation) % top, axis=1)


def shares(amount, total, limit, skew, full):
    weights = [(1 << 20) // math.isqrt(standing ** skew) + 1 for standing in range(1, amount + 1)]
    largest = limit if full else min(limit, max(-(-total // amount), total * weights[0] // sum(weights)))
    least = 1 if total - largest >= amount - 1 else 0
    given, rest = [largest] + [least] * (amount - 1), total - largest - least * (amount - 1)
    while rest > 0:
        candidates = [i for i in range(1, amount) if given[i] < largest] or [i for i in range(1, amount) if given[i] < limit]
        pool, budget = sum([weights[i] for i in candidates]), rest
        for i in candidates:
            extra = min(limit - given[i], max(1, budget * weights[i] // pool), rest)
            given[i] = given[i] + extra
            rest = rest - extra
    return np.array(given)


def scatter_about(rng, extent, deviation, limit, cuts=(), kind=jnp.bfloat16):
    values = deviation * jax.random.normal(rng, extent, jnp.float32)
    if cuts:
        values = values * shard_levels(rng, extent, cuts, -0.22, 0.18)
    return jnp.clip(values, -limit, limit).astype(kind)


def setup_inputs(seed: int = 0) -> dict:
    splits = jax.random.split(jax.random.key(seed), 10)
    queries = draw_queries(jax.random.fold_in(splits[9], 71), 0)
    rotated_key_rows = draw_rotated_key_rows(jax.random.fold_in(splits[9], 71), 0)
    value_row_array = scatter_about(splits[2], (N_EXP, GROUP_TOKENS, KEY_VALUE_HEADS * HEAD_SIZE), 1.0, 6.0, ((0, 2), (1, 16)))
    residual = draw_residual(jax.random.fold_in(splits[9], 71), 0)
    norm_gain = jnp.clip(1.0 + 0.18 * jax.random.normal(splits[4], (D,), jnp.float32), 0.1, 1.9)
    expert_ids_keys = jax.random.split(jax.random.fold_in(splits[5], 1), N_EXP * GROUP_TOKENS // TOK_DEV)
    expert_ids_turns = jax.random.permutation(jax.random.fold_in(splits[5], 3), N_EXP * GROUP_TOKENS // TOK_DEV)
    expert_ids = jax.vmap(lambda own, number: assign_block(jax.random.fold_in(splits[5], 2), own, number, TOK_DEV, EXPERTS, TOP, MOST, 2))(expert_ids_keys, expert_ids_turns).reshape((N_EXP, GROUP_TOKENS, TOP))
    gate_values = jnp.clip(0.25 + 0.75 * jax.random.uniform(splits[6], (N_EXP, GROUP_TOKENS, TOP), jnp.float32) ** shard_levels(splits[6], (N_EXP, GROUP_TOKENS, TOP), ((0, 2), (1, 16)), -0.2, 0.2), 0.25, 1.0)
    w_gate_up = scatter_about(splits[7], (N_CTX, N_EXP, 2, QUARTER, D), D ** -0.5, 0.125, ((0, 16), (1, 2)))
    w_down = scatter_about(splits[8], (N_CTX, N_EXP, QUARTER, D), HID ** -0.5, 0.21875, ((0, 16), (1, 2)))
    return dict(queries=queries, rotated_key_rows=rotated_key_rows, value_row_array=value_row_array, residual=residual, norm_gain=norm_gain, expert_ids=expert_ids, gate_values=gate_values, w_gate_up=w_gate_up, w_down=w_down)


def to_prompts(array):
    width = array.shape[-1]
    split = array.reshape(N_EXP, N_CTX // 2, 2, TOK_DEV, width)
    return jnp.transpose(split, (0, 2, 1, 3, 4)).reshape(N_EXP * 2, PROMPT_LENGTH, width)

def from_prompts(array):
    width = array.shape[-1]
    split = array.reshape(N_EXP, 2, N_CTX // 2, TOK_DEV, width)
    return jnp.transpose(split, (0, 2, 1, 3, 4)).reshape(N_EXP, GROUP_TOKENS, width)

def attend_whole_prompt(operands):
    queries, rotated_key_rows, value_row_array = operands
    queries_per_key_head = QUERY_HEADS // KEY_VALUE_HEADS
    block_length = math.gcd(PROMPT_LENGTH, 512)
    query_head_rows = queries.reshape(PROMPT_LENGTH // block_length, block_length, KEY_VALUE_HEADS, queries_per_key_head, HEAD_SIZE).astype(jnp.float32)
    key_head_rows = rotated_key_rows.reshape(PROMPT_LENGTH, KEY_VALUE_HEADS, HEAD_SIZE).astype(jnp.float32)
    value_head_rows = value_row_array.reshape(PROMPT_LENGTH, KEY_VALUE_HEADS, HEAD_SIZE).astype(jnp.float32)
    key_pos = jnp.arange(PROMPT_LENGTH, dtype=jnp.int32)

    def one_block(pair):
        query_block, block_index = pair
        scores = jnp.einsum('qhgd,khd->hgqk', query_block, key_head_rows) / math.sqrt(HEAD_SIZE)
        query_pos = block_index * block_length + jnp.arange(block_length, dtype=jnp.int32)
        allowed = key_pos[None, :] <= query_pos[:, None]
        scores = jnp.where(allowed, scores, -1e+30)
        row_peak = lax.optimization_barrier(jnp.max(scores, axis=-1, keepdims=True))
        expo_vals = jnp.exp(scores - row_peak)
        row_total = lax.optimization_barrier(jnp.sum(expo_vals, axis=-1))
        rounded = lax.optimization_barrier(expo_vals.astype(jnp.bfloat16))
        weights = rounded.astype(jnp.float32)
        summed = jnp.einsum('hgqk,khd->qhgd', weights, value_head_rows)
        return summed / jnp.transpose(row_total, (2, 0, 1))[..., None]
    result = lax.map(one_block, (query_head_rows, jnp.arange(PROMPT_LENGTH // block_length, dtype=jnp.int32)))
    return result.reshape(PROMPT_LENGTH, QUERY_HEADS * HEAD_SIZE)

def reference(queries, rotated_key_rows, value_row_array, residual, norm_gain, expert_ids, gate_values, w_gate_up, w_down):
    attended_rows = lax.map(attend_whole_prompt, (to_prompts(queries), to_prompts(rotated_key_rows), to_prompts(value_row_array)))
    attended_rows = from_prompts(attended_rows)
    mid_rows = (residual.astype(jnp.float32) + attended_rows).astype(jnp.bfloat16)
    mid_wide = mid_rows.astype(jnp.float32)
    inverse = lax.rsqrt(lax.optimization_barrier(jnp.mean(mid_wide * mid_wide, axis=-1, keepdims=True)) + 1e-06)
    normed = (mid_wide * inverse * norm_gain.astype(jnp.float32)).astype(jnp.bfloat16)
    token_count = N_EXP * GROUP_TOKENS
    flat_rows = normed.reshape(token_count, D)
    assign_count = token_count * TOP
    routed = expert_ids.reshape(assign_count).astype(jnp.int32)
    order = jnp.argsort(routed, stable=True).astype(jnp.int32)
    counts = jax.ops.segment_sum(jnp.ones(assign_count, jnp.int32), routed, num_segments=EXPERTS).astype(jnp.int32)
    starts = (jnp.cumsum(counts) - counts).astype(jnp.int32)
    capacity = N_CTX * N_EXP * MOST
    order = jnp.concatenate([order, jnp.zeros(capacity, jnp.int32)])
    zero_index = jnp.zeros((), jnp.int32)

    def one_expert(carried, expert):
        chosen = lax.dynamic_slice(order, (starts[expert],), (capacity,))
        live = jnp.arange(capacity, dtype=jnp.int32) < counts[expert]
        inputs = flat_rows[chosen // TOP]
        group_index = (expert // EPG).astype(jnp.int32)
        local_index = (expert % EPG).astype(jnp.int32)
        gate_up = lax.dynamic_slice(w_gate_up, (local_index * 4, group_index, zero_index, zero_index, zero_index), (4, 1, 2, QUARTER, D))[:, 0]
        down_rows = lax.dynamic_slice(w_down, (local_index * 4, group_index, zero_index, zero_index), (4, 1, QUARTER, D))[:, 0]
        summed = jnp.zeros((capacity, D), jnp.float32)
        for quarter in range(4):
            projected = lax.dot_general(gate_up[quarter], inputs, (((2,), (1,)), ((), ())), preferred_element_type=jnp.float32)
            hidden = (jax.nn.silu(projected[0]) * projected[1]).astype(jnp.bfloat16)
            part_out = lax.dot_general(hidden, down_rows[quarter], (((0,), (0,)), ((), ())), preferred_element_type=jnp.float32).astype(jnp.bfloat16)
            summed = summed + part_out.astype(jnp.float32)
        target = jnp.where(live, chosen, assign_count)
        carried = carried.at[target].set(summed.astype(jnp.bfloat16), mode='drop')
        return (carried, None)
    gathered, _ = lax.scan(one_expert, jnp.zeros((assign_count, D), jnp.bfloat16), jnp.arange(EXPERTS, dtype=jnp.int32))
    expert_out = gathered.reshape(token_count, TOP, D).astype(jnp.float32)
    gated = gate_values.reshape(token_count, TOP, 1).astype(jnp.float32) * expert_out
    layer_out = (mid_rows.reshape(token_count, D).astype(jnp.float32) + lax.optimization_barrier(jnp.sum(gated, axis=1))).astype(jnp.bfloat16)
    return layer_out.reshape(N_EXP, GROUP_TOKENS, D)
```

```python
import functools
import math

import jax
import jax.numpy as jnp
from jax import lax
from jax.experimental import pallas as pl
from jax.experimental.pallas import tpu as pltpu
from jax.sharding import PartitionSpec as P

QUERY_HEADS = 16
KEY_VALUE_HEADS = 2
HEAD_SIZE = 128
GROUP_HEADS = QUERY_HEADS // KEY_VALUE_HEADS
KV_WIDTH = KEY_VALUE_HEADS * HEAD_SIZE
NEGATIVE_FILL = -1e30
MESH = pl.DeviceIdType.MESH
NT = (((1,), (1,)), ((), ()))


def layer_kernel(
    ctx_count,
    exp_count,
    slot_depth,
    q_ref,
    k_ref,
    v_ref,
    res_ref,
    gain_ref,
    ids_ref,
    gate_ref,
    wgu_ref,
    wdn_ref,
    out_ref,
    kvbuf,
    peak,
    total,
    acc,
    mid,
    weights,
    outgoing,
    incoming,
    returned,
    local_sem,
    kv_send,
    kv_recv,
    w_send,
    w_recv,
    d_send,
    d_recv,
    r_send,
    r_recv,
):
    tokens, width = q_ref.shape
    quarter = wdn_ref.shape[0]
    ctx = lax.axis_index("ctx")
    exp = lax.axis_index("exp")
    prompt_devs = ctx_count // 2
    prompt = lax.rem(ctx, 2)
    in_prompt = ctx // 2
    per_group = ctx_count // 4
    experts = per_group * exp_count
    place = lax.rem(ctx, 4)
    quad = ctx - place
    own_expert = exp * per_group + ctx // 4
    sibling_place = place + 1 - 2 * lax.rem(place, 2)
    neighbour_place = lax.rem(place + 2, 4)
    sibling = (quad + sibling_place, exp)
    neighbour = (quad + neighbour_place, exp)

    def holder(expert):
        return (lax.rem(expert, per_group) * 4 + place, expert // per_group)

    barrier = pltpu.get_barrier_semaphore()

    def greet(device):
        pl.semaphore_signal(barrier, inc=1, device_id=device, device_id_type=MESH)

    @pl.loop(1, prompt_devs)
    def _(step):
        greet((lax.rem(in_prompt + step, prompt_devs) * 2 + prompt, exp))

    greet(sibling)

    @pl.loop(0, per_group * (exp_count - 1))
    def _(index):
        other = lax.rem(exp + 1 + index // per_group, exp_count)
        greet((lax.rem(index, per_group) * 4 + place, other))

    kvbuf[0, :, :KV_WIDTH] = k_ref[...]
    kvbuf[0, :, KV_WIDTH:] = v_ref[...]
    pl.semaphore_wait(barrier, prompt_devs + per_group * (exp_count - 1))

    def kv_copy(step):
        return pltpu.make_async_remote_copy(
            src_ref=kvbuf.at[0],
            dst_ref=kvbuf.at[step],
            send_sem=kv_send.at[step],
            recv_sem=kv_recv.at[step],
            device_id=((in_prompt + step) * 2 + prompt, exp),
            device_id_type=MESH,
        )

    @pl.loop(1, prompt_devs - in_prompt)
    def _(back):
        kv_copy(prompt_devs - in_prompt - back).start()

    def weight_source(part):
        return wgu_ref.at[part] if part < 2 else wdn_ref

    def weight_rows(part, whose):
        return weights.at[part, pl.ds(pl.multiple_of(whose * quarter, 16), quarter)]

    def weight_copy(part, route):
        whose = neighbour_place if route == 2 else place
        return pltpu.make_async_remote_copy(
            src_ref=weight_rows(part, whose) if route == 2 else weight_source(part),
            dst_ref=weight_rows(part, whose),
            send_sem=w_send.at[route, part],
            recv_sem=w_recv.at[route, part],
            device_id=neighbour if route == 1 else sibling,
            device_id_type=MESH,
        )

    def weight_arrival(part, route):
        whose = (sibling_place, neighbour_place, lax.rem(sibling_place + 2, 4))[route]
        rows = weight_rows(part, whose)
        return pltpu.make_async_remote_copy(
            src_ref=rows,
            dst_ref=rows,
            send_sem=w_send.at[route, part],
            recv_sem=w_recv.at[route, part],
            device_id=sibling,
            device_id_type=MESH,
        )

    def weight_local(part):
        return pltpu.make_async_copy(
            weight_source(part), weight_rows(part, place), local_sem.at[part]
        )

    for part in range(3):
        weight_copy(part, 1).start()
    for part in range(3):
        weight_local(part).start()
        weight_copy(part, 0).start()

    scale = 1.0 / math.sqrt(HEAD_SIZE)

    def attend(slot, first):
        for group in range(KEY_VALUE_HEADS):
            columns = slice(group * HEAD_SIZE, (group + 1) * HEAD_SIZE)
            value_columns = slice(KV_WIDTH + group * HEAD_SIZE, KV_WIDTH + (group + 1) * HEAD_SIZE)
            keys = kvbuf[slot, :, columns]
            values = kvbuf[slot, :, value_columns]
            base = group * GROUP_HEADS
            for head in range(base, base + GROUP_HEADS):
                query = q_ref[:, head * HEAD_SIZE : (head + 1) * HEAD_SIZE]
                scores = lax.dot_general(query, keys, NT, preferred_element_type=jnp.float32)
                scores = scores * scale
                if first:
                    row = lax.broadcasted_iota(jnp.int32, scores.shape, 0)
                    column = lax.broadcasted_iota(jnp.int32, scores.shape, 1)
                    scores = jnp.where(row >= column, scores, NEGATIVE_FILL)
                new_peak = jnp.max(scores, axis=1, keepdims=True)
                if not first:
                    old_peak = peak[head]
                    new_peak = jnp.maximum(old_peak, new_peak)
                expo = jnp.exp(scores - new_peak)
                row_sum = jnp.sum(expo, axis=1, keepdims=True)
                summed = jnp.dot(
                    expo.astype(jnp.bfloat16), values, preferred_element_type=jnp.float32
                )
                if first:
                    total[head] = row_sum
                    acc[head] = summed
                else:
                    factor = jnp.exp(old_peak - new_peak)
                    total[head] = total[head] * factor + row_sum
                    acc[head] = acc[head] * factor + summed
                peak[head] = new_peak

    attend(0, True)

    ids = ids_ref[...]
    lanes = -(-experts // 128) * 128
    onehot = (ids == lax.broadcasted_iota(jnp.int32, (tokens, lanes), 1)).astype(jnp.float32)
    earlier = (
        lax.broadcasted_iota(jnp.int32, (tokens, tokens), 0)
        > lax.broadcasted_iota(jnp.int32, (tokens, tokens), 1)
    ).astype(jnp.float32)
    before = jnp.dot(
        earlier.astype(jnp.bfloat16), onehot.astype(jnp.bfloat16), preferred_element_type=jnp.float32
    )
    rank = jnp.sum(before * onehot, axis=1, keepdims=True)
    slot = ids.astype(jnp.float32) * slot_depth + rank
    slot_lanes = jnp.transpose(jnp.broadcast_to(slot, (tokens, tokens)))[:1, :]

    @pl.loop(1, in_prompt + 1)
    def _(step):
        kv_copy(step).wait_recv()
        attend(step, False)

    for head in range(QUERY_HEADS):
        columns = slice(head * HEAD_SIZE, (head + 1) * HEAD_SIZE)
        attended = acc[head] / total[head]
        mid[:, columns] = (res_ref[:, columns].astype(jnp.float32) + attended).astype(jnp.bfloat16)
    mid_wide = mid[...].astype(jnp.float32)
    inverse = lax.rsqrt(jnp.mean(mid_wide * mid_wide, axis=1, keepdims=True) + 1e-06)
    normed = (mid_wide * inverse * gain_ref[...]).astype(jnp.bfloat16)

    slots = experts * slot_depth
    chunk = min(slots, 256)
    for start in range(0, slots, chunk):
        number = (lax.broadcasted_iota(jnp.int32, (chunk, tokens), 0) + start).astype(jnp.float32)
        pick = (number == slot_lanes).astype(jnp.float32).astype(jnp.bfloat16)
        outgoing[start : start + chunk] = jnp.dot(
            pick, normed, preferred_element_type=jnp.float32
        ).astype(jnp.bfloat16)

    def slot_rows(ref, expert):
        return ref.at[pl.ds(pl.multiple_of(expert * slot_depth, 16), slot_depth)]

    def ahead(step):
        return lax.rem(own_expert + step, experts)

    def behind(step):
        return lax.rem(own_expert + experts - step, experts)

    def dispatch(step):
        return pltpu.make_async_remote_copy(
            src_ref=slot_rows(outgoing, ahead(step)),
            dst_ref=slot_rows(incoming, own_expert),
            send_sem=d_send.at[step],
            recv_sem=d_recv.at[step],
            device_id=holder(ahead(step)),
            device_id_type=MESH,
        )

    def dispatched(step):
        rows = slot_rows(incoming, behind(step))
        return pltpu.make_async_remote_copy(
            src_ref=rows,
            dst_ref=rows,
            send_sem=d_send.at[step],
            recv_sem=d_recv.at[step],
            device_id=holder(behind(step)),
            device_id_type=MESH,
        )

    def give_back(step):
        return pltpu.make_async_remote_copy(
            src_ref=slot_rows(incoming, behind(step)),
            dst_ref=slot_rows(returned, own_expert),
            send_sem=r_send.at[step],
            recv_sem=r_recv.at[step],
            device_id=holder(behind(step)),
            device_id_type=MESH,
        )

    def given_back(step):
        rows = slot_rows(returned, ahead(step))
        return pltpu.make_async_remote_copy(
            src_ref=rows,
            dst_ref=rows,
            send_sem=r_send.at[step],
            recv_sem=r_recv.at[step],
            device_id=holder(ahead(step)),
            device_id_type=MESH,
        )

    @pl.loop(1, experts)
    def _(step):
        dispatch(step).start()

    own_rows = pl.ds(pl.multiple_of(own_expert * slot_depth, 16), slot_depth)
    incoming[own_rows] = outgoing[own_rows]

    for part in range(3):
        weight_arrival(part, 1).wait_recv()
        weight_copy(part, 2).start()

    @pl.loop(1, experts)
    def _(step):
        dispatched(step).wait_recv()

    for part in range(3):
        weight_local(part).wait()
        weight_arrival(part, 0).wait_recv()
        weight_arrival(part, 2).wait_recv()

    def expert_chunk(start):
        rows = incoming[pl.ds(start, chunk)]
        gate = lax.dot_general(rows, weights[0], NT, preferred_element_type=jnp.float32)
        up = lax.dot_general(rows, weights[1], NT, preferred_element_type=jnp.float32)
        hidden = (gate / (1.0 + jnp.exp(-gate)) * up).astype(jnp.bfloat16)
        incoming[pl.ds(start, chunk)] = jnp.dot(
            hidden, weights[2], preferred_element_type=jnp.float32
        ).astype(jnp.bfloat16)

    if slots == chunk:
        expert_chunk(0)
    else:

        @pl.loop(0, slots // chunk)
        def _(index):
            expert_chunk(pl.multiple_of(index * chunk, chunk))

    @pl.loop(1, experts)
    def _(step):
        give_back(step).start()

    returned[own_rows] = incoming[own_rows]

    @pl.loop(1, prompt_devs - in_prompt)
    def _(step):
        kv_copy(step).wait_send()

    for part in range(3):
        for route in range(3):
            weight_copy(part, route).wait_send()

    @pl.loop(1, experts)
    def _(step):
        dispatch(step).wait_send()

    @pl.loop(1, experts)
    def _(step):
        given_back(step).wait_recv()

    number = lax.broadcasted_iota(jnp.int32, (tokens, slots), 1).astype(jnp.float32)
    place_back = (number == slot).astype(jnp.float32).astype(jnp.bfloat16)
    expert_out = jnp.dot(place_back, returned[...], preferred_element_type=jnp.float32)
    out_ref[...] = (mid[...].astype(jnp.float32) + gate_ref[...] * expert_out).astype(jnp.bfloat16)

    @pl.loop(1, experts)
    def _(step):
        give_back(step).wait_send()


def on_device(
    queries,
    rotated_key_rows,
    value_row_array,
    residual,
    norm_gain,
    expert_ids,
    gate_values,
    w_gate_up,
    w_down,
):
    ctx_count = lax.axis_size("ctx")
    exp_count = lax.axis_size("exp")
    tokens, width = queries.shape[1:]
    quarter = w_down.shape[2]
    prompt_devs = ctx_count // 2
    experts = ctx_count // 4 * exp_count
    slot_depth = max(2, 2 * tokens // experts)
    slot_depth = -(-slot_depth // 16) * 16
    slots = experts * slot_depth
    vmem = pl.BlockSpec(memory_space=pltpu.VMEM)
    dma = pltpu.SemaphoreType.DMA
    out = pl.pallas_call(
        functools.partial(layer_kernel, ctx_count, exp_count, slot_depth),
        out_shape=jax.ShapeDtypeStruct((tokens, width), jnp.bfloat16),
        in_specs=[vmem] * 7 + [pl.BlockSpec(memory_space=pl.ANY)] * 2,
        out_specs=vmem,
        scratch_shapes=[
            pltpu.VMEM((prompt_devs, tokens, 2 * KV_WIDTH), jnp.bfloat16),
            pltpu.VMEM((QUERY_HEADS, tokens, 1), jnp.float32),
            pltpu.VMEM((QUERY_HEADS, tokens, 1), jnp.float32),
            pltpu.VMEM((QUERY_HEADS, tokens, HEAD_SIZE), jnp.float32),
            pltpu.VMEM((tokens, width), jnp.bfloat16),
            pltpu.VMEM((3, 4 * quarter, width), jnp.bfloat16),
            pltpu.VMEM((slots, width), jnp.bfloat16),
            pltpu.VMEM((slots, width), jnp.bfloat16),
            pltpu.VMEM((slots, width), jnp.bfloat16),
            dma((3,)),
            dma((prompt_devs,)),
            dma((prompt_devs,)),
            dma((3, 3)),
            dma((3, 3)),
            dma((experts,)),
            dma((experts,)),
            dma((experts,)),
            dma((experts,)),
        ],
        compiler_params=pltpu.CompilerParams(
            collective_id=0, has_side_effects=True, vmem_limit_bytes=58 * 1024 * 1024
        ),
    )(
        queries[0],
        rotated_key_rows[0],
        value_row_array[0],
        residual[0],
        norm_gain[None],
        expert_ids[0],
        gate_values[0],
        w_gate_up[0, 0],
        w_down[0, 0],
    )
    return out[None]


def solution(mesh):
    return jax.shard_map(
        on_device,
        mesh=mesh,
        in_specs=(
            P("exp", "ctx", None),
            P("exp", "ctx", None),
            P("exp", "ctx", None),
            P("exp", "ctx", None),
            P(),
            P("exp", "ctx", None),
            P("exp", "ctx", None),
            P("ctx", "exp", None, None, None),
            P("ctx", "exp", None, None),
        ),
        out_specs=P("exp", "ctx", None),
        check_vma=False,
    )
```

```python
import functools
import math

import jax
import jax.numpy as jnp
from jax import lax
from jax.experimental import pallas as pl
from jax.experimental.pallas import tpu as pltpu
from jax.sharding import PartitionSpec as P

QUERY_HEADS = 16
KEY_VALUE_HEADS = 2
HEAD_SIZE = 128
GROUP_HEADS = QUERY_HEADS // KEY_VALUE_HEADS
KV_WIDTH = KEY_VALUE_HEADS * HEAD_SIZE
NEGATIVE_FILL = -1e30
MESH = pl.DeviceIdType.MESH
NT = (((1,), (1,)), ((), ()))


def layer_kernel(
    ctx_count,
    exp_count,
    slot_depth,
    q_ref,
    k_ref,
    v_ref,
    res_ref,
    gain_ref,
    ids_ref,
    gate_ref,
    wgu_ref,
    wdn_ref,
    out_ref,
    kvbuf,
    stacked,
    peak,
    total,
    acc,
    mid,
    weights,
    outgoing,
    incoming,
    returned,
    local_sem,
    kv_send,
    kv_recv,
    w_send,
    w_recv,
    d_send,
    d_recv,
    r_send,
    r_recv,
):
    tokens, width = q_ref.shape
    quarter = wdn_ref.shape[0]
    ctx = lax.axis_index("ctx")
    exp = lax.axis_index("exp")
    prompt_devs = ctx_count // 2
    prompt = lax.rem(ctx, 2)
    in_prompt = ctx // 2
    per_group = ctx_count // 4
    experts = per_group * exp_count
    place = lax.rem(ctx, 4)
    quad = ctx - place
    own_expert = exp * per_group + ctx // 4
    sibling_place = place + 1 - 2 * lax.rem(place, 2)
    neighbour_place = lax.rem(place + 2, 4)
    sibling = (quad + sibling_place, exp)
    neighbour = (quad + neighbour_place, exp)

    def holder(expert):
        return (lax.rem(expert, per_group) * 4 + place, expert // per_group)

    barrier = pltpu.get_barrier_semaphore()

    def greet(device):
        pl.semaphore_signal(barrier, inc=1, device_id=device, device_id_type=MESH)

    @pl.loop(1, prompt_devs)
    def _(step):
        greet((lax.rem(in_prompt + step, prompt_devs) * 2 + prompt, exp))

    greet(sibling)

    @pl.loop(0, per_group * (exp_count - 1))
    def _(index):
        other = lax.rem(exp + 1 + index // per_group, exp_count)
        greet((lax.rem(index, per_group) * 4 + place, other))

    kvbuf[0, :, :KV_WIDTH] = k_ref[...]
    for group in range(KEY_VALUE_HEADS):
        columns = slice(group * HEAD_SIZE, (group + 1) * HEAD_SIZE)
        value_columns = slice(KV_WIDTH + group * HEAD_SIZE, KV_WIDTH + (group + 1) * HEAD_SIZE)
        kvbuf[0, :, value_columns] = jnp.transpose(v_ref[:, columns].astype(jnp.float32)).astype(
            jnp.bfloat16
        )
    pl.semaphore_wait(barrier, prompt_devs + per_group * (exp_count - 1))

    level = in_prompt // 2
    side = lax.rem(in_prompt, 2)
    is_last = level + 1 == prompt_devs // 2

    def kv_swap():
        return pltpu.make_async_remote_copy(
            src_ref=kvbuf.at[0],
            dst_ref=kvbuf.at[1],
            send_sem=kv_send.at[prompt_devs],
            recv_sem=kv_recv.at[1],
            device_id=neighbour,
            device_id_type=MESH,
        )

    def kv_up(index):
        return pltpu.make_async_remote_copy(
            src_ref=kvbuf.at[index],
            dst_ref=kvbuf.at[index + 2],
            send_sem=kv_send.at[index],
            recv_sem=kv_recv.at[index + 2],
            device_id=(ctx + 4, exp),
            device_id_type=MESH,
        )

    def kv_arrival(index):
        return pltpu.make_async_remote_copy(
            src_ref=kvbuf.at[index],
            dst_ref=kvbuf.at[index],
            send_sem=kv_send.at[index],
            recv_sem=kv_recv.at[index],
            device_id=neighbour,
            device_id_type=MESH,
        )

    kv_swap().start()

    @pl.when(jnp.logical_not(is_last))
    def _():
        kv_up(0).start()

    def weight_source(part):
        return wgu_ref.at[part] if part < 2 else wdn_ref

    def weight_rows(part, whose):
        return weights.at[part, pl.ds(pl.multiple_of(whose * quarter, 16), quarter)]

    def weight_copy(part, route):
        whose = neighbour_place if route == 2 else place
        return pltpu.make_async_remote_copy(
            src_ref=weight_rows(part, whose) if route == 2 else weight_source(part),
            dst_ref=weight_rows(part, whose),
            send_sem=w_send.at[route, part],
            recv_sem=w_recv.at[route, part],
            device_id=neighbour if route == 1 else sibling,
            device_id_type=MESH,
        )

    def weight_arrival(part, route):
        whose = (sibling_place, neighbour_place, lax.rem(sibling_place + 2, 4))[route]
        rows = weight_rows(part, whose)
        return pltpu.make_async_remote_copy(
            src_ref=rows,
            dst_ref=rows,
            send_sem=w_send.at[route, part],
            recv_sem=w_recv.at[route, part],
            device_id=sibling,
            device_id_type=MESH,
        )

    def weight_local(part):
        return pltpu.make_async_copy(
            weight_source(part), weight_rows(part, place), local_sem.at[part]
        )

    for part in range(3):
        weight_copy(part, 1).start()
    for part in range(3):
        weight_local(part).start()
        weight_copy(part, 0).start()

    for head in range(QUERY_HEADS):
        stacked[head * tokens : (head + 1) * tokens] = q_ref[
            :, head * HEAD_SIZE : (head + 1) * HEAD_SIZE
        ]
    scale = math.log2(math.e) / math.sqrt(HEAD_SIZE)
    span = GROUP_HEADS * tokens

    def attend(slot, first):
        for group in range(KEY_VALUE_HEADS):
            lanes = slice(group * span, (group + 1) * span)
            columns = slice(group * HEAD_SIZE, (group + 1) * HEAD_SIZE)
            value_columns = slice(KV_WIDTH + group * HEAD_SIZE, KV_WIDTH + (group + 1) * HEAD_SIZE)
            scores = lax.dot_general(
                kvbuf[slot, :, columns], stacked[lanes], NT, preferred_element_type=jnp.float32
            )
            if first:
                key = lax.broadcasted_iota(jnp.int32, scores.shape, 0)
                query = lax.rem(lax.broadcasted_iota(jnp.int32, scores.shape, 1), tokens)
                scores = jnp.where(key <= query, scores, NEGATIVE_FILL)
            new_peak = jnp.max(scores, axis=0, keepdims=True)
            if not first:
                old_peak = peak[:, lanes]
                new_peak = jnp.maximum(old_peak, new_peak)
            expo = jnp.exp2((scores - new_peak) * scale)
            row_sum = jnp.sum(expo, axis=0, keepdims=True)
            summed = jnp.dot(
                kvbuf[slot, :, value_columns],
                expo.astype(jnp.bfloat16),
                preferred_element_type=jnp.float32,
            )
            if first:
                total[:, lanes] = row_sum
                acc[:, lanes] = summed
            else:
                factor = jnp.exp2((old_peak - new_peak) * scale)
                total[:, lanes] = total[:, lanes] * factor + row_sum
                acc[:, lanes] = acc[:, lanes] * factor + summed
            peak[:, lanes] = new_peak

    attend(0, True)

    ids = ids_ref[...]
    lanes = -(-experts // 128) * 128
    onehot = (ids == lax.broadcasted_iota(jnp.int32, (tokens, lanes), 1)).astype(jnp.float32)
    earlier = (
        lax.broadcasted_iota(jnp.int32, (tokens, tokens), 0)
        > lax.broadcasted_iota(jnp.int32, (tokens, tokens), 1)
    ).astype(jnp.float32)
    before = jnp.dot(
        earlier.astype(jnp.bfloat16), onehot.astype(jnp.bfloat16), preferred_element_type=jnp.float32
    )
    rank = jnp.sum(before * onehot, axis=1, keepdims=True)
    slot = ids.astype(jnp.float32) * slot_depth + rank
    slot_lanes = jnp.transpose(jnp.broadcast_to(slot, (tokens, tokens)))[:1, :]

    @pl.loop(1, 2 * level + 2)
    def _(index):
        kv_arrival(index).wait_recv()

        @pl.when(jnp.logical_not(is_last))
        def _():
            kv_up(index).start()

        @pl.when(jnp.logical_or(index > 1, side == 1))
        def _():
            attend(index, False)

    for head in range(QUERY_HEADS):
        columns = slice(head * HEAD_SIZE, (head + 1) * HEAD_SIZE)
        lanes = slice(head * tokens, (head + 1) * tokens)
        attended = jnp.transpose(acc[:, lanes] / total[:, lanes])
        mid[:, columns] = (res_ref[:, columns].astype(jnp.float32) + attended).astype(jnp.bfloat16)
    mid_wide = mid[...].astype(jnp.float32)
    inverse = lax.rsqrt(jnp.mean(mid_wide * mid_wide, axis=1, keepdims=True) + 1e-06)
    normed = (mid_wide * inverse * gain_ref[...]).astype(jnp.bfloat16)

    slots = experts * slot_depth
    chunk = min(slots, 256)
    for start in range(0, slots, chunk):
        number = (lax.broadcasted_iota(jnp.int32, (chunk, tokens), 0) + start).astype(jnp.float32)
        pick = (number == slot_lanes).astype(jnp.float32).astype(jnp.bfloat16)
        outgoing[start : start + chunk] = jnp.dot(
            pick, normed, preferred_element_type=jnp.float32
        ).astype(jnp.bfloat16)

    def slot_rows(ref, expert):
        return ref.at[pl.ds(pl.multiple_of(expert * slot_depth, 16), slot_depth)]

    def ahead(step):
        return lax.rem(own_expert + step, experts)

    def behind(step):
        return lax.rem(own_expert + experts - step, experts)

    def dispatch(step):
        return pltpu.make_async_remote_copy(
            src_ref=slot_rows(outgoing, ahead(step)),
            dst_ref=slot_rows(incoming, own_expert),
            send_sem=d_send.at[step],
            recv_sem=d_recv.at[step],
            device_id=holder(ahead(step)),
            device_id_type=MESH,
        )

    def dispatched(step):
        rows = slot_rows(incoming, behind(step))
        return pltpu.make_async_remote_copy(
            src_ref=rows,
            dst_ref=rows,
            send_sem=d_send.at[step],
            recv_sem=d_recv.at[step],
            device_id=holder(behind(step)),
            device_id_type=MESH,
        )

    def give_back(step):
        return pltpu.make_async_remote_copy(
            src_ref=slot_rows(incoming, behind(step)),
            dst_ref=slot_rows(returned, own_expert),
            send_sem=r_send.at[step],
            recv_sem=r_recv.at[step],
            device_id=holder(behind(step)),
            device_id_type=MESH,
        )

    def given_back(step):
        rows = slot_rows(returned, ahead(step))
        return pltpu.make_async_remote_copy(
            src_ref=rows,
            dst_ref=rows,
            send_sem=r_send.at[step],
            recv_sem=r_recv.at[step],
            device_id=holder(ahead(step)),
            device_id_type=MESH,
        )

    @pl.loop(1, experts)
    def _(step):
        dispatch(step).start()

    own_rows = pl.ds(pl.multiple_of(own_expert * slot_depth, 16), slot_depth)
    incoming[own_rows] = outgoing[own_rows]

    def hand_on(part):
        weight_arrival(part, 1).wait_recv()
        weight_copy(part, 2).start()

    hand_on(0)
    hand_on(1)

    @pl.loop(1, experts)
    def _(step):
        dispatched(step).wait_recv()

    def await_weights(part):
        if part == 2:
            hand_on(part)
        weight_local(part).wait()
        weight_arrival(part, 0).wait_recv()
        weight_arrival(part, 2).wait_recv()

    await_weights(0)
    await_weights(1)
    if slots > chunk:
        await_weights(2)

    def expert_chunk(start):
        rows = incoming[pl.ds(start, chunk)]
        gate = lax.dot_general(rows, weights[0], NT, preferred_element_type=jnp.float32)
        up = lax.dot_general(rows, weights[1], NT, preferred_element_type=jnp.float32)
        hidden = (gate / (1.0 + jnp.exp(-gate)) * up).astype(jnp.bfloat16)
        if slots == chunk:
            await_weights(2)
        incoming[pl.ds(start, chunk)] = jnp.dot(
            hidden, weights[2], preferred_element_type=jnp.float32
        ).astype(jnp.bfloat16)

    if slots == chunk:
        expert_chunk(0)
    else:

        @pl.loop(0, slots // chunk)
        def _(index):
            expert_chunk(pl.multiple_of(index * chunk, chunk))

    @pl.loop(1, experts)
    def _(step):
        give_back(step).start()

    returned[own_rows] = incoming[own_rows]

    kv_swap().wait_send()

    @pl.when(jnp.logical_not(is_last))
    def _():
        @pl.loop(0, 2 * level + 2)
        def _(index):
            kv_up(index).wait_send()

    for part in range(3):
        for route in range(3):
            weight_copy(part, route).wait_send()

    @pl.loop(1, experts)
    def _(step):
        dispatch(step).wait_send()

    @pl.loop(1, experts)
    def _(step):
        given_back(step).wait_recv()

    number = lax.broadcasted_iota(jnp.int32, (tokens, slots), 1).astype(jnp.float32)
    place_back = (number == slot).astype(jnp.float32).astype(jnp.bfloat16)
    expert_out = jnp.dot(place_back, returned[...], preferred_element_type=jnp.float32)
    out_ref[...] = (mid[...].astype(jnp.float32) + gate_ref[...] * expert_out).astype(jnp.bfloat16)

    @pl.loop(1, experts)
    def _(step):
        give_back(step).wait_send()


def on_device(
    queries,
    rotated_key_rows,
    value_row_array,
    residual,
    norm_gain,
    expert_ids,
    gate_values,
    w_gate_up,
    w_down,
):
    ctx_count = lax.axis_size("ctx")
    exp_count = lax.axis_size("exp")
    tokens, width = queries.shape[1:]
    quarter = w_down.shape[2]
    prompt_devs = ctx_count // 2
    experts = ctx_count // 4 * exp_count
    slot_depth = max(2, 2 * tokens // experts)
    slot_depth = -(-slot_depth // 16) * 16
    slots = experts * slot_depth
    vmem = pl.BlockSpec(memory_space=pltpu.VMEM)
    dma = pltpu.SemaphoreType.DMA
    out = pl.pallas_call(
        functools.partial(layer_kernel, ctx_count, exp_count, slot_depth),
        out_shape=jax.ShapeDtypeStruct((tokens, width), jnp.bfloat16),
        in_specs=[vmem] * 7 + [pl.BlockSpec(memory_space=pl.ANY)] * 2,
        out_specs=vmem,
        scratch_shapes=[
            pltpu.VMEM((prompt_devs, tokens, 2 * KV_WIDTH), jnp.bfloat16),
            pltpu.VMEM((QUERY_HEADS * tokens, HEAD_SIZE), jnp.bfloat16),
            pltpu.VMEM((1, QUERY_HEADS * tokens), jnp.float32),
            pltpu.VMEM((1, QUERY_HEADS * tokens), jnp.float32),
            pltpu.VMEM((HEAD_SIZE, QUERY_HEADS * tokens), jnp.float32),
            pltpu.VMEM((tokens, width), jnp.bfloat16),
            pltpu.VMEM((3, 4 * quarter, width), jnp.bfloat16),
            pltpu.VMEM((slots, width), jnp.bfloat16),
            pltpu.VMEM((slots, width), jnp.bfloat16),
            pltpu.VMEM((slots, width), jnp.bfloat16),
            dma((3,)),
            dma((prompt_devs + 1,)),
            dma((prompt_devs,)),
            dma((3, 3)),
            dma((3, 3)),
            dma((experts,)),
            dma((experts,)),
            dma((experts,)),
            dma((experts,)),
        ],
        compiler_params=pltpu.CompilerParams(
            collective_id=0, has_side_effects=True, vmem_limit_bytes=58 * 1024 * 1024
        ),
    )(
        queries[0],
        rotated_key_rows[0],
        value_row_array[0],
        residual[0],
        norm_gain[None],
        expert_ids[0],
        gate_values[0],
        w_gate_up[0, 0],
        w_down[0, 0],
    )
    return out[None]


def solution(mesh):
    return jax.shard_map(
        on_device,
        mesh=mesh,
        in_specs=(
            P("exp", "ctx", None),
            P("exp", "ctx", None),
            P("exp", "ctx", None),
            P("exp", "ctx", None),
            P(),
            P("exp", "ctx", None),
            P("exp", "ctx", None),
            P("ctx", "exp", None, None, None),
            P("ctx", "exp", None, None),
        ),
        out_specs=P("exp", "ctx", None),
        check_vma=False,
    )
```

```python
import functools
import math

import jax
import jax.numpy as jnp
from jax import lax
from jax.experimental import pallas as pl
from jax.experimental.pallas import tpu as pltpu
from jax.sharding import PartitionSpec as P

QUERY_HEADS = 16
KEY_VALUE_HEADS = 2
HEAD_SIZE = 128
GROUP_HEADS = QUERY_HEADS // KEY_VALUE_HEADS
KV_WIDTH = KEY_VALUE_HEADS * HEAD_SIZE
NEGATIVE_FILL = -1e30
MESH = pl.DeviceIdType.MESH
NT = (((1,), (1,)), ((), ()))


def layer_kernel(
    ctx_count,
    exp_count,
    slot_depth,
    q_ref,
    k_ref,
    v_ref,
    res_ref,
    gain_ref,
    ids_ref,
    gate_ref,
    wgu_ref,
    wdn_ref,
    out_ref,
    kvbuf,
    stacked,
    peak,
    total,
    acc,
    mid,
    weights,
    outgoing,
    incoming,
    returned,
    local_sem,
    kv_send,
    kv_recv,
    w_send,
    w_recv,
    d_send,
    d_recv,
    r_send,
    r_recv,
):
    tokens, width = q_ref.shape
    quarter = wdn_ref.shape[0]
    ctx = lax.axis_index("ctx")
    exp = lax.axis_index("exp")
    prompt_devs = ctx_count // 2
    prompt = lax.rem(ctx, 2)
    in_prompt = ctx // 2
    per_group = ctx_count // 4
    experts = per_group * exp_count
    place = lax.rem(ctx, 4)
    quad = ctx - place
    own_expert = exp * per_group + ctx // 4
    sibling_place = place + 1 - 2 * lax.rem(place, 2)
    neighbour_place = lax.rem(place + 2, 4)
    sibling = (quad + sibling_place, exp)
    neighbour = (quad + neighbour_place, exp)

    def holder(expert):
        return (lax.rem(expert, per_group) * 4 + place, expert // per_group)

    barrier = pltpu.get_barrier_semaphore()

    def greet(device):
        pl.semaphore_signal(barrier, inc=1, device_id=device, device_id_type=MESH)

    @pl.loop(1, prompt_devs)
    def _(step):
        greet((lax.rem(in_prompt + step, prompt_devs) * 2 + prompt, exp))

    greet(sibling)

    @pl.loop(0, per_group * (exp_count - 1))
    def _(index):
        other = lax.rem(exp + 1 + index // per_group, exp_count)
        greet((lax.rem(index, per_group) * 4 + place, other))

    kvbuf[0, :, :KV_WIDTH] = k_ref[...]
    for group in range(KEY_VALUE_HEADS):
        columns = slice(group * HEAD_SIZE, (group + 1) * HEAD_SIZE)
        value_columns = slice(KV_WIDTH + group * HEAD_SIZE, KV_WIDTH + (group + 1) * HEAD_SIZE)
        kvbuf[0, :, value_columns] = jnp.transpose(v_ref[:, columns].astype(jnp.float32)).astype(
            jnp.bfloat16
        )
    pl.semaphore_wait(barrier, prompt_devs + per_group * (exp_count - 1))

    level = in_prompt // 2
    side = lax.rem(in_prompt, 2)
    is_last = level + 1 == prompt_devs // 2

    def kv_swap():
        return pltpu.make_async_remote_copy(
            src_ref=kvbuf.at[0],
            dst_ref=kvbuf.at[1],
            send_sem=kv_send.at[prompt_devs],
            recv_sem=kv_recv.at[1],
            device_id=neighbour,
            device_id_type=MESH,
        )

    def kv_up(index):
        return pltpu.make_async_remote_copy(
            src_ref=kvbuf.at[index],
            dst_ref=kvbuf.at[index + 2],
            send_sem=kv_send.at[index],
            recv_sem=kv_recv.at[index + 2],
            device_id=(ctx + 4, exp),
            device_id_type=MESH,
        )

    def kv_arrival(index):
        return pltpu.make_async_remote_copy(
            src_ref=kvbuf.at[index],
            dst_ref=kvbuf.at[index],
            send_sem=kv_send.at[index],
            recv_sem=kv_recv.at[index],
            device_id=neighbour,
            device_id_type=MESH,
        )

    kv_swap().start()

    @pl.when(jnp.logical_not(is_last))
    def _():
        kv_up(0).start()

    def weight_source(part):
        return wgu_ref.at[part] if part < 2 else wdn_ref

    def weight_rows(part, whose):
        return weights.at[part, pl.ds(pl.multiple_of(whose * quarter, 16), quarter)]

    def weight_copy(part, route):
        whose = neighbour_place if route == 2 else place
        return pltpu.make_async_remote_copy(
            src_ref=weight_rows(part, whose) if route == 2 else weight_source(part),
            dst_ref=weight_rows(part, whose),
            send_sem=w_send.at[route, part],
            recv_sem=w_recv.at[route, part],
            device_id=neighbour if route == 1 else sibling,
            device_id_type=MESH,
        )

    def weight_arrival(part, route):
        whose = (sibling_place, neighbour_place, lax.rem(sibling_place + 2, 4))[route]
        rows = weight_rows(part, whose)
        return pltpu.make_async_remote_copy(
            src_ref=rows,
            dst_ref=rows,
            send_sem=w_send.at[route, part],
            recv_sem=w_recv.at[route, part],
            device_id=sibling,
            device_id_type=MESH,
        )

    def weight_local(part):
        return pltpu.make_async_copy(
            weight_source(part), weight_rows(part, place), local_sem.at[part]
        )

    for part in range(3):
        weight_copy(part, 1).start()
    for part in range(3):
        weight_local(part).start()
        weight_copy(part, 0).start()

    for head in range(QUERY_HEADS):
        stacked[head * tokens : (head + 1) * tokens] = q_ref[
            :, head * HEAD_SIZE : (head + 1) * HEAD_SIZE
        ]
    scale = math.log2(math.e) / math.sqrt(HEAD_SIZE)
    span = GROUP_HEADS * tokens

    def attend(slot, first):
        for group in range(KEY_VALUE_HEADS):
            lanes = slice(group * span, (group + 1) * span)
            columns = slice(group * HEAD_SIZE, (group + 1) * HEAD_SIZE)
            value_columns = slice(KV_WIDTH + group * HEAD_SIZE, KV_WIDTH + (group + 1) * HEAD_SIZE)
            scores = lax.dot_general(
                kvbuf[slot, :, columns], stacked[lanes], NT, preferred_element_type=jnp.float32
            )
            if first:
                key = lax.broadcasted_iota(jnp.int32, scores.shape, 0)
                query = lax.rem(lax.broadcasted_iota(jnp.int32, scores.shape, 1), tokens)
                scores = jnp.where(key <= query, scores, NEGATIVE_FILL)
            new_peak = jnp.max(scores, axis=0, keepdims=True)
            if not first:
                old_peak = peak[:, lanes]
                new_peak = jnp.maximum(old_peak, new_peak)
            expo = jnp.exp2((scores - new_peak) * scale)
            row_sum = jnp.sum(expo, axis=0, keepdims=True)
            summed = jnp.dot(
                kvbuf[slot, :, value_columns],
                expo.astype(jnp.bfloat16),
                preferred_element_type=jnp.float32,
            )
            if first:
                total[:, lanes] = row_sum
                acc[:, lanes] = summed
            else:
                factor = jnp.exp2((old_peak - new_peak) * scale)
                total[:, lanes] = total[:, lanes] * factor + row_sum
                acc[:, lanes] = acc[:, lanes] * factor + summed
            peak[:, lanes] = new_peak

    attend(0, True)

    def down_rows(row):
        return jnp.transpose(jnp.broadcast_to(row, (tokens, tokens)))[:, :1]

    ids = down_rows(ids_ref[...].astype(jnp.float32))
    gates = down_rows(gate_ref[...])
    lanes = -(-experts // 128) * 128
    onehot = (
        ids == lax.broadcasted_iota(jnp.int32, (tokens, lanes), 1).astype(jnp.float32)
    ).astype(jnp.float32)
    earlier = (
        lax.broadcasted_iota(jnp.int32, (tokens, tokens), 0)
        > lax.broadcasted_iota(jnp.int32, (tokens, tokens), 1)
    ).astype(jnp.float32)
    before = jnp.dot(
        earlier.astype(jnp.bfloat16), onehot.astype(jnp.bfloat16), preferred_element_type=jnp.float32
    )
    rank = jnp.sum(before * onehot, axis=1, keepdims=True)
    slot = ids * slot_depth + rank
    slot_lanes = jnp.transpose(jnp.broadcast_to(slot, (tokens, tokens)))[:1, :]

    @pl.loop(1, 2 * level + 2)
    def _(index):
        kv_arrival(index).wait_recv()

        @pl.when(jnp.logical_not(is_last))
        def _():
            kv_up(index).start()

        @pl.when(jnp.logical_or(index > 1, side == 1))
        def _():
            attend(index, False)

    for head in range(QUERY_HEADS):
        columns = slice(head * HEAD_SIZE, (head + 1) * HEAD_SIZE)
        lanes = slice(head * tokens, (head + 1) * tokens)
        attended = jnp.transpose(acc[:, lanes] / total[:, lanes])
        mid[:, columns] = (res_ref[:, columns].astype(jnp.float32) + attended).astype(jnp.bfloat16)
    mid_wide = mid[...].astype(jnp.float32)
    inverse = lax.rsqrt(jnp.mean(mid_wide * mid_wide, axis=1, keepdims=True) + 1e-06)
    normed = (mid_wide * inverse * gain_ref[...]).astype(jnp.bfloat16)

    slots = experts * slot_depth
    chunk = min(slots, 256)
    for start in range(0, slots, chunk):
        number = (lax.broadcasted_iota(jnp.int32, (chunk, tokens), 0) + start).astype(jnp.float32)
        pick = (number == slot_lanes).astype(jnp.float32).astype(jnp.bfloat16)
        outgoing[start : start + chunk] = jnp.dot(
            pick, normed, preferred_element_type=jnp.float32
        ).astype(jnp.bfloat16)

    def slot_rows(ref, expert):
        return ref.at[pl.ds(pl.multiple_of(expert * slot_depth, 16), slot_depth)]

    def ahead(step):
        return lax.rem(own_expert + step, experts)

    def behind(step):
        return lax.rem(own_expert + experts - step, experts)

    def dispatch(step):
        return pltpu.make_async_remote_copy(
            src_ref=slot_rows(outgoing, ahead(step)),
            dst_ref=slot_rows(incoming, own_expert),
            send_sem=d_send.at[step],
            recv_sem=d_recv.at[step],
            device_id=holder(ahead(step)),
            device_id_type=MESH,
        )

    def dispatched(step):
        rows = slot_rows(incoming, behind(step))
        return pltpu.make_async_remote_copy(
            src_ref=rows,
            dst_ref=rows,
            send_sem=d_send.at[step],
            recv_sem=d_recv.at[step],
            device_id=holder(behind(step)),
            device_id_type=MESH,
        )

    def give_back(step):
        return pltpu.make_async_remote_copy(
            src_ref=slot_rows(incoming, behind(step)),
            dst_ref=slot_rows(returned, own_expert),
            send_sem=r_send.at[step],
            recv_sem=r_recv.at[step],
            device_id=holder(behind(step)),
            device_id_type=MESH,
        )

    def given_back(step):
        rows = slot_rows(returned, ahead(step))
        return pltpu.make_async_remote_copy(
            src_ref=rows,
            dst_ref=rows,
            send_sem=r_send.at[step],
            recv_sem=r_recv.at[step],
            device_id=holder(ahead(step)),
            device_id_type=MESH,
        )

    @pl.loop(1, experts)
    def _(step):
        dispatch(step).start()

    own_rows = pl.ds(pl.multiple_of(own_expert * slot_depth, 16), slot_depth)
    incoming[own_rows] = outgoing[own_rows]

    def hand_on(part):
        weight_arrival(part, 1).wait_recv()
        weight_copy(part, 2).start()

    hand_on(0)
    hand_on(1)

    @pl.loop(1, experts)
    def _(step):
        dispatched(step).wait_recv()

    def await_weights(part):
        if part == 2:
            hand_on(part)
        weight_local(part).wait()
        weight_arrival(part, 0).wait_recv()
        weight_arrival(part, 2).wait_recv()

    await_weights(0)
    await_weights(1)
    if slots > chunk:
        await_weights(2)

    def expert_chunk(start):
        rows = incoming[pl.ds(start, chunk)]
        gate = lax.dot_general(rows, weights[0], NT, preferred_element_type=jnp.float32)
        up = lax.dot_general(rows, weights[1], NT, preferred_element_type=jnp.float32)
        hidden = (gate / (1.0 + jnp.exp(-gate)) * up).astype(jnp.bfloat16)
        if slots == chunk:
            await_weights(2)
        incoming[pl.ds(start, chunk)] = jnp.dot(
            hidden, weights[2], preferred_element_type=jnp.float32
        ).astype(jnp.bfloat16)

    if slots == chunk:
        expert_chunk(0)
    else:

        @pl.loop(0, slots // chunk)
        def _(index):
            expert_chunk(pl.multiple_of(index * chunk, chunk))

    @pl.loop(1, experts)
    def _(step):
        give_back(step).start()

    returned[own_rows] = incoming[own_rows]

    kv_swap().wait_send()

    @pl.when(jnp.logical_not(is_last))
    def _():
        @pl.loop(0, 2 * level + 2)
        def _(index):
            kv_up(index).wait_send()

    for part in range(3):
        for route in range(3):
            weight_copy(part, route).wait_send()

    @pl.loop(1, experts)
    def _(step):
        dispatch(step).wait_send()

    @pl.loop(1, experts)
    def _(step):
        given_back(step).wait_recv()

    number = lax.broadcasted_iota(jnp.int32, (tokens, slots), 1).astype(jnp.float32)
    place_back = (number == slot).astype(jnp.float32).astype(jnp.bfloat16)
    expert_out = jnp.dot(place_back, returned[...], preferred_element_type=jnp.float32)
    out_ref[...] = (mid[...].astype(jnp.float32) + gates * expert_out).astype(jnp.bfloat16)

    @pl.loop(1, experts)
    def _(step):
        give_back(step).wait_send()


def on_device(
    queries,
    rotated_key_rows,
    value_row_array,
    residual,
    norm_gain,
    expert_ids,
    gate_values,
    w_gate_up,
    w_down,
):
    ctx_count = lax.axis_size("ctx")
    exp_count = lax.axis_size("exp")
    tokens, width = queries.shape[1:]
    quarter = w_down.shape[2]
    prompt_devs = ctx_count // 2
    experts = ctx_count // 4 * exp_count
    slot_depth = max(2, 2 * tokens // experts)
    slot_depth = -(-slot_depth // 16) * 16
    slots = experts * slot_depth
    vmem = pl.BlockSpec(memory_space=pltpu.VMEM)
    dma = pltpu.SemaphoreType.DMA
    out = pl.pallas_call(
        functools.partial(layer_kernel, ctx_count, exp_count, slot_depth),
        out_shape=jax.ShapeDtypeStruct((tokens, width), jnp.bfloat16),
        in_specs=[vmem] * 7 + [pl.BlockSpec(memory_space=pl.ANY)] * 2,
        out_specs=vmem,
        scratch_shapes=[
            pltpu.VMEM((prompt_devs, tokens, 2 * KV_WIDTH), jnp.bfloat16),
            pltpu.VMEM((QUERY_HEADS * tokens, HEAD_SIZE), jnp.bfloat16),
            pltpu.VMEM((1, QUERY_HEADS * tokens), jnp.float32),
            pltpu.VMEM((1, QUERY_HEADS * tokens), jnp.float32),
            pltpu.VMEM((HEAD_SIZE, QUERY_HEADS * tokens), jnp.float32),
            pltpu.VMEM((tokens, width), jnp.bfloat16),
            pltpu.VMEM((3, 4 * quarter, width), jnp.bfloat16),
            pltpu.VMEM((slots, width), jnp.bfloat16),
            pltpu.VMEM((slots, width), jnp.bfloat16),
            pltpu.VMEM((slots, width), jnp.bfloat16),
            dma((3,)),
            dma((prompt_devs + 1,)),
            dma((prompt_devs,)),
            dma((3, 3)),
            dma((3, 3)),
            dma((experts,)),
            dma((experts,)),
            dma((experts,)),
            dma((experts,)),
        ],
        compiler_params=pltpu.CompilerParams(
            collective_id=0, has_side_effects=True, vmem_limit_bytes=58 * 1024 * 1024
        ),
    )(
        queries[0],
        rotated_key_rows[0],
        value_row_array[0],
        residual[0],
        norm_gain[None],
        expert_ids.reshape(1, tokens),
        gate_values.reshape(1, tokens),
        w_gate_up[0, 0],
        w_down[0, 0],
    )
    return out[None]


def solution(mesh):
    return jax.shard_map(
        on_device,
        mesh=mesh,
        in_specs=(
            P("exp", "ctx", None),
            P("exp", "ctx", None),
            P("exp", "ctx", None),
            P("exp", "ctx", None),
            P(),
            P("exp", "ctx", None),
            P("exp", "ctx", None),
            P("ctx", "exp", None, None, None),
            P("ctx", "exp", None, None),
        ),
        out_specs=P("exp", "ctx", None),
        check_vma=False,
    )
```
